32 devices in a mesh: dp: 2 (over core), ctx: 16 (over z, y, x).
Axes of the slice: x: 2, y: 2, z: 4, core: 2. Of those that a mesh axis runs over, the one named last changes fastest.
Arguments:
- hidden: bfloat16 [4, 2048, 5376], P('dp', 'ctx'), parts along dimension 0, may hold values from -400 to 400
- queries: bfloat16 [4, 2048, 2048], P('dp', 'ctx'), parts along dimension 0, may hold values from -400 to 400
- input_gain: float32 [5376], replicated, may hold values from 0.1 to 1.9
- kv_weight: bfloat16 [5376, 2048], P('ctx'), may hold values from -0.078125 to 0.078125
- query_gain: float32 [128], replicated, may hold values from 1 to 2.5
- key_gain: float32 [128], replicated, may hold values from 1 to 2.5
Outputs:
- attended: bfloat16 [4, 2048, 2048], P('dp', 'ctx'), parts along dimension 0
The draws below stay inside these ranges and needn't reach their ends.
There are 2 independent parts, one for each index of `dp`. The reference program is written for one: setup_inputs(seed, part) draws one part's arguments, and reference() takes and returns one part's arrays. A program takes and returns all parts, laid end to end along the dimension named above; an argument that names none is the same for every part. Nothing has to cross between parts.
All inputs are finite; a program needn't handle non-finite values.
Results may differ from the reference program's by a relative error of at most 0.012.
Values may be sent and summed in bfloat16 or wider, within the bound.
No kernel may reach another device: no remote copies, remote signals or barrier semaphores. Data moves between devices by JAX's collectives and lax.ppermute only.
A program may use at most 128 MiB of HBM per device.

```python
import math
import jax
import jax.numpy as jnp
from jax import lax

D = 5376
QH = 16
KVH = 8
HD = 128
WINDOW = 1024
TOK_DEV = 128
SEQS = 2
LENGTH = 2048


def scaled_field(key, field_shape):
    base_key, row_key, column_key = jax.random.split(key, 3)
    row_shape = field_shape[:-1] + (1,)
    base_values = jax.random.truncated_normal(base_key, -4.0, 4.0, field_shape, jnp.float32)
    row_scale = jnp.exp(jax.random.uniform(row_key, row_shape, jnp.float32, 0.0, math.log(10.0)))
    column_scale = jnp.exp(jax.random.uniform(column_key, (field_shape[-1],), jnp.float32, 0.0, math.log(10.0)))
    return (base_values * row_scale * column_scale).astype(jnp.bfloat16)


def draw_hidden(key, part):
    return scaled_field(jax.random.fold_in(key, 11), (SEQS, LENGTH, D))


def draw_queries(key, part):
    return scaled_field(jax.random.fold_in(key, 23), (SEQS, LENGTH, QH * HD))


def steps_of(rng, shape, pieces, low, largest):
    def one(dim, shards_of):
        heights = jax.random.uniform(jax.random.fold_in(jax.random.fold_in(rng, 6), dim), (shards_of,), jnp.float32, low / len(pieces), largest / len(pieces))
        return jnp.repeat(jnp.exp(heights), shape[dim] // shards_of).reshape((-1,) + (1,) * (len(shape) - dim - 1))

    factor_of = one(*pieces[0])
    for cut in pieces[1:]:
        factor_of = factor_of * one(*cut)
    return factor_of


def normal_values(own_key, extent, scale, limit, pieces=(), held_as=jnp.bfloat16):
    entries = jax.random.normal(own_key, extent, jnp.float32) * scale
    if len(pieces) > 0:
        entries = steps_of(own_key, extent, pieces, -0.22, 0.18) * entries
    return jnp.clip(entries, min=-limit, max=limit).astype(held_as)


def setup_inputs(seed: int = 0, part: int = 0) -> dict:
    splits = jax.random.split(jax.random.key(seed), 7)
    part_keys = jax.random.split(jax.random.fold_in(splits[6], part), 7)
    hidden = draw_hidden(jax.random.fold_in(jax.random.fold_in(splits[6], part), 71), part)
    queries = draw_queries(jax.random.fold_in(jax.random.fold_in(splits[6], part), 71), part)
    input_gain = jnp.clip(1.0 + 0.18 * jax.random.normal(splits[2], (D,), jnp.float32), 0.1, 1.9)
    kv_weight = normal_values(splits[3], (D, 2 * KVH * HD), D ** -0.5, 0.078125, ((0, 16),))
    query_gain = jnp.clip(jnp.exp(jax.random.uniform(splits[4], (HD,), jnp.float32, math.log(1.0), math.log(2.5))), 1.0, 2.5)
    key_gain = jnp.clip(jnp.exp(jax.random.uniform(splits[5], (HD,), jnp.float32, math.log(1.0), math.log(2.5))), 1.0, 2.5)
    return dict(hidden=hidden, queries=queries, input_gain=input_gain, kv_weight=kv_weight, query_gain=query_gain, key_gain=key_gain)


attn_scalar = 168.0
norm_eps = 1e-06

def rotary_tables(positions, head_width):
    half_width = head_width // 2
    exponent = 2.0 * jnp.arange(half_width, dtype=jnp.float32) / head_width
    inverse = jnp.power(10000.0, -exponent)
    angles = positions.astype(jnp.float32)[:, None] * inverse[None, :]
    return (jnp.cos(angles), jnp.sin(angles))

def rotate(heads, cos_table, sine_table):
    half_width = heads.shape[-1] // 2
    first = heads[..., :half_width]
    second = heads[..., half_width:]
    cos_part = cos_table[:, None, :]
    sine_part = sine_table[:, None, :]
    return jnp.concatenate([first * cos_part - second * sine_part, second * cos_part + first * sine_part], axis=-1)

def head_norm(heads, gain):
    return heads * lax.rsqrt(lax.optimization_barrier(jnp.mean(heads * heads, axis=-1, keepdims=True)) + norm_eps) * gain

def reference(hidden, queries, input_gain, kv_weight, query_gain, key_gain):
    kv_half = KVH * HD
    group_size = QH // KVH
    results = []
    for seq_index in range(SEQS):
        hidden_f32 = hidden[seq_index].astype(jnp.float32)
        normed = (hidden_f32 * lax.rsqrt(lax.optimization_barrier(jnp.mean(hidden_f32 * hidden_f32, axis=-1, keepdims=True)) + norm_eps) * input_gain).astype(jnp.bfloat16)
        projected = jnp.dot(normed, kv_weight, preferred_element_type=jnp.float32)
        positions = jnp.arange(LENGTH, dtype=jnp.int32)
        cos_table, sine_table = rotary_tables(positions, HD)
        key_rows = rotate(head_norm(projected[:, :kv_half].reshape(LENGTH, KVH, HD), key_gain), cos_table, sine_table)
        key_rows = lax.optimization_barrier(key_rows.astype(jnp.bfloat16))
        value_rows = lax.optimization_barrier(projected[:, kv_half:].reshape(LENGTH, KVH, HD).astype(jnp.bfloat16))
        query_f32 = queries[seq_index].astype(jnp.float32).reshape(LENGTH, QH, HD)
        query_rows = rotate(head_norm(query_f32, query_gain), cos_table, sine_table) * attn_scalar ** (-0.5)
        query_rows = lax.optimization_barrier(query_rows.astype(jnp.bfloat16))
        padded_keys = jnp.pad(key_rows, ((WINDOW, 0), (0, 0), (0, 0)))
        padded_values = jnp.pad(value_rows, ((WINDOW, 0), (0, 0), (0, 0)))

        def one_block(block_index):
            row_start = (block_index * TOK_DEV).astype(jnp.int32)
            query_block = lax.dynamic_slice_in_dim(query_rows, row_start, TOK_DEV, 0).reshape(TOK_DEV, KVH, group_size, HD)
            near_keys = lax.dynamic_slice_in_dim(padded_keys, row_start, WINDOW + TOK_DEV, 0)
            near_values = lax.dynamic_slice_in_dim(padded_values, row_start, WINDOW + TOK_DEV, 0)
            query_pos = row_start + jnp.arange(TOK_DEV, dtype=jnp.int32)
            key_pos = row_start - WINDOW + jnp.arange(WINDOW + TOK_DEV, dtype=jnp.int32)
            allowed = (key_pos[None, :] <= query_pos[:, None]) & (key_pos[None, :] > query_pos[:, None] - WINDOW) & (key_pos[None, :] >= 0)
            scores = jnp.einsum('qhgd,khd->hgqk', query_block.astype(jnp.float32), near_keys.astype(jnp.float32))
            weights = jnp.where(allowed, jnp.exp(scores), 0.0)
            row_total = lax.optimization_barrier(jnp.sum(weights, axis=-1))
            rounded = lax.optimization_barrier(weights.astype(jnp.bfloat16)).astype(jnp.float32)
            weighted = jnp.einsum('hgqk,khd->qhgd', rounded, near_values.astype(jnp.float32))
            result = weighted / jnp.transpose(row_total, (2, 0, 1))[..., None]
            return result.astype(jnp.bfloat16).reshape(TOK_DEV, QH * HD)
        blocks = lax.map(one_block, jnp.arange(LENGTH // TOK_DEV, dtype=jnp.int32))
        results.append(blocks.reshape(LENGTH, QH * HD))
    return jnp.stack(results, axis=0)
```

```python
import functools

import jax
import jax.numpy as jnp
from jax import lax
from jax.experimental import pallas as pl
from jax.experimental.pallas import tpu as pltpu
from jax.sharding import PartitionSpec as P

HD = 128
WINDOW = 1024
QUAD = 4

attn_scalar = 168.0
norm_eps = 1e-06
F32 = jnp.float32
BF16 = jnp.bfloat16
MIB = 1 << 20


def params(mib, grid_dims=0):
    sem = ("arbitrary",) * grid_dims if grid_dims else None
    return pltpu.CompilerParams(vmem_limit_bytes=mib * MIB, dimension_semantics=sem)


SMEM = pl.BlockSpec(memory_space=pltpu.SMEM)
VMEM = pl.BlockSpec(memory_space=pltpu.VMEM)


def rotary_tables(positions, head_width):
    half_width = head_width // 2
    exponent = 2.0 * jnp.arange(half_width, dtype=F32) / head_width
    inverse = jnp.power(10000.0, -exponent)
    angles = positions.astype(F32)[:, None] * inverse[None, :]
    cos, sin = jnp.cos(angles), jnp.sin(angles)
    return jnp.concatenate([cos, cos], axis=1), jnp.concatenate([-sin, sin], axis=1)


def norm_rotate(u, gain, cos, sin):
    scaled = u * lax.rsqrt(jnp.mean(u * u, axis=-1, keepdims=True) + norm_eps) * gain
    return scaled * cos + pltpu.roll(scaled, HD // 2, 1) * sin


def norm_kernel(slices, width, sc, x_ref, g_ref, *refs):
    outs, scratch = refs[:QUAD], refs[QUAD]
    x = x_ref[...].astype(F32)
    y = x * lax.rsqrt(jnp.mean(x * x, axis=-1, keepdims=True) + norm_eps) * g_ref[...]
    y = y.astype(BF16)
    for i in range(slices):
        at = (i // QUAD) * width
        scratch[i % QUAD, :, at : at + width] = y[:, i * width : (i + 1) * width]
    for m in range(QUAD):
        outs[m][...] = scratch[sc[0] ^ m]


def norm_slices(sc, x, gain, shard_rows):
    rows, width = x.shape
    part = width // QUAD
    step = rows // 4
    return pl.pallas_call(
        functools.partial(norm_kernel, width // shard_rows, shard_rows),
        grid=(4,),
        in_specs=[
            SMEM,
            pl.BlockSpec((step, width), lambda i: (i, 0)),
            pl.BlockSpec((1, width), lambda i: (0, 0)),
        ],
        out_specs=[pl.BlockSpec((step, part), lambda i: (i, 0))] * QUAD,
        out_shape=[jax.ShapeDtypeStruct((rows, part), BF16)] * QUAD,
        scratch_shapes=[pltpu.VMEM((QUAD, step, part), BF16)],
        compiler_params=params(32, 1),
        name="norm_slices",
    )(sc, x, gain.reshape(1, width))


def query_kernel(seqs, sc, q_ref, g_ref, cos_ref, sin_ref, *outs):
    width = outs[0].shape[1]
    length = cos_ref.shape[0]
    for m in range(QUAD):
        at = pl.multiple_of((sc[0] ^ m) * width, width)
        for s in range(seqs):
            for h in range(width // HD):
                u = q_ref[pl.ds(s * length, length), pl.ds(at + h * HD, HD)].astype(F32)
                y = norm_rotate(u, g_ref[...], cos_ref[...], sin_ref[...])
                y = y * attn_scalar ** (-0.5)
                outs[m][s * length : (s + 1) * length, h * HD : (h + 1) * HD] = y.astype(BF16)


def query_slots(sc, q, gain, cos, sin, seqs):
    rows, width = q.shape
    return pl.pallas_call(
        functools.partial(query_kernel, seqs),
        in_specs=[SMEM, VMEM, VMEM, VMEM, VMEM],
        out_specs=[VMEM] * QUAD,
        out_shape=[jax.ShapeDtypeStruct((rows, width // QUAD), BF16)] * QUAD,
        compiler_params=params(16),
        name="query_slots",
    )(sc, q, gain.reshape(1, HD), cos, sin)


def project_kernel(pieces, sc, *refs):
    xs, refs = refs[:QUAD], refs[QUAD:]
    ws, refs = refs[: 2 * pieces], refs[2 * pieces :]
    outs, scratch = refs[:QUAD], refs[QUAD]
    rows = ws[0].shape[0]
    core = sc[1]
    for k in range(pieces):
        at = pl.multiple_of(sc[3 + k] * rows, 16)
        for side in range(2):
            for q in range(QUAD):
                scratch[q, core ^ side, pl.ds(at, rows), :] = ws[2 * k + side][
                    :, q * HD : (q + 1) * HD
                ]
    for m in range(QUAD):
        q = sc[0] ^ m
        w = jnp.concatenate([scratch[q, 0], scratch[q, 1]], axis=1)
        for d in range(QUAD):
            y = jnp.dot(xs[d][...], w, preferred_element_type=F32)
            outs[m][m ^ d] = y.astype(outs[m].dtype)


def project(sc, xs, ws):
    rows, depth = xs[0].shape
    pieces = len(ws) // 2
    shape = (QUAD, rows, 2 * HD)
    return pl.pallas_call(
        functools.partial(project_kernel, pieces),
        in_specs=[SMEM] + [VMEM] * (QUAD + 2 * pieces),
        out_specs=[VMEM] * QUAD,
        out_shape=[jax.ShapeDtypeStruct(shape, F32)]
        + [jax.ShapeDtypeStruct(shape, BF16)] * (QUAD - 1),
        scratch_shapes=[pltpu.VMEM((QUAD, 2, depth, HD), BF16)],
        compiler_params=params(40),
        name="project",
    )(sc, *xs, *ws)


def reduce_kernel(seqs, own_ref, *refs):
    parts, refs = refs[: QUAD - 1], refs[QUAD - 1 :]
    g_ref, cos_ref, sin_ref, out_ref = refs
    length = cos_ref.shape[1]
    total = own_ref[0]
    for part in parts:
        total = total + part[0].astype(F32)
    for s in range(seqs):
        at = slice(s * length, (s + 1) * length)
        key = norm_rotate(total[at, :HD], g_ref[...], cos_ref[0], sin_ref[0])
        out_ref[0, at, :HD] = key.astype(BF16)
        out_ref[0, at, HD:] = total[at, HD:].astype(BF16)


def reduce_parts(parts, gain, cos, sin, seqs):
    _, rows, width = parts[0].shape
    block = pl.BlockSpec((1, rows, width), lambda e: (e, 0, 0))
    table = pl.BlockSpec((1,) + cos.shape[1:], lambda e: (e, 0, 0))
    return pl.pallas_call(
        functools.partial(reduce_kernel, seqs),
        grid=(QUAD,),
        in_specs=[block] * QUAD + [pl.BlockSpec((1, HD), lambda e: (0, 0)), table, table],
        out_specs=block,
        out_shape=jax.ShapeDtypeStruct(parts[0].shape, BF16),
        compiler_params=params(16, 1),
        name="reduce_parts",
    )(*parts, gain.reshape(1, HD), cos, sin)


def attend_kernel(layers, sc, *refs):
    qs, refs = refs[:QUAD], refs[QUAD:]
    kvs, refs = refs[:layers], refs[layers:]
    outs, refs = refs[:QUAD], refs[QUAD:]
    q_scr, k_scr, v_scr, o_scr = refs
    r, layer = sc[0], sc[2]
    length = qs[0].shape[0]
    heads = qs[0].shape[1] // HD
    span = QUAD * length
    for m in range(QUAD):
        for h in range(heads):
            q_scr[r ^ m, h * length : (h + 1) * length] = qs[m][:, h * HD : (h + 1) * HD]
    for back in range(layers):
        for j in range(QUAD):
            at = (layers - 1 - back) * span + j * length
            kv = kvs[back][r ^ j]
            k_scr[at : at + length] = kv[:, :HD]
            v_scr[at : at + length] = kv[:, HD:]
    shape = (heads * length, length)
    row = lax.broadcasted_iota(jnp.int32, (heads, length, length), 1).reshape(shape)
    column = lax.broadcasted_iota(jnp.int32, shape, 1)

    def attend(back):
        for i in range(QUAD):
            stop = (layers - 1) * span + (i + 1) * length
            start = (layers - 1 - back) * span
            windowed = stop - length - WINDOW >= start
            if windowed:
                start = stop - length - WINDOW
            scores = lax.dot_general(
                q_scr[i],
                k_scr[start:stop],
                (((1,), (1,)), ((), ())),
                preferred_element_type=F32,
            )
            weights = jnp.exp(scores)
            blocks = [weights[:, :-length], jnp.where(column <= row, weights[:, -length:], 0.0)]
            if windowed:
                blocks[0] = jnp.concatenate(
                    [jnp.where(column > row, weights[:, :length], 0.0), blocks[0][:, length:]], axis=1
                )
            if blocks[0].shape[1] == 0:
                blocks = blocks[1:]
            weights = jnp.concatenate(blocks, axis=1)
            total = jnp.sum(weights, axis=-1, keepdims=True)
            out = jnp.dot(weights.astype(BF16), v_scr[start:stop], preferred_element_type=F32)
            out = (out / total).astype(BF16)
            for h in range(heads):
                o_scr[i, :, h * HD : (h + 1) * HD] = out[h * length : (h + 1) * length]

    for back in range(layers):
        here = layer == back if back < layers - 1 else layer >= back
        pl.when(here)(functools.partial(attend, back))
    for m in range(QUAD):
        outs[m][...] = o_scr[r ^ m]


def attend(sc, qs, kvs, chunk, chunks, seqs):
    rows, width = qs[0].shape
    width = width // chunks
    length = rows // seqs
    layers = len(kvs)
    heads = width // HD
    return pl.pallas_call(
        functools.partial(attend_kernel, layers),
        grid=(seqs,),
        in_specs=[SMEM]
        + [pl.BlockSpec((length, width), lambda s: (s, chunk))] * QUAD
        + [pl.BlockSpec((QUAD, length, 2 * HD), lambda s: (0, s, 0))] * layers,
        out_specs=[pl.BlockSpec((length, width), lambda s: (s, 0))] * QUAD,
        out_shape=[jax.ShapeDtypeStruct((rows, width), BF16)] * QUAD,
        scratch_shapes=[
            pltpu.VMEM((QUAD, heads * length, HD), BF16),
            pltpu.VMEM((layers * QUAD * length, HD), BF16),
            pltpu.VMEM((layers * QUAD * length, HD), BF16),
            pltpu.VMEM((QUAD, length, width), BF16),
        ],
        compiler_params=params(32, 1),
        name="attend",
    )(sc, *qs, *kvs)


def assemble_kernel(chunks, sc, *refs):
    out = refs[-1]
    width = refs[0].shape[1]
    for m in range(QUAD):
        for a in range(chunks):
            at = pl.multiple_of(((sc[0] ^ m) * chunks + a) * width, width)
            out[:, pl.ds(at, width)] = refs[m * chunks + a][...]


def assemble(sc, slots, chunks):
    rows, width = slots[0].shape
    return pl.pallas_call(
        functools.partial(assemble_kernel, chunks),
        in_specs=[SMEM] + [VMEM] * len(slots),
        out_specs=VMEM,
        out_shape=jax.ShapeDtypeStruct((rows, width * len(slots)), BF16),
        compiler_params=params(16),
        name="assemble",
    )(sc, *slots)


def body(hidden, queries, input_gain, kv_weight, query_gain, key_gain):
    seqs, length, model_width = hidden.shape
    shard_rows, kv_width = kv_weight.shape
    devices = lax.axis_size("ctx")
    layers_total = devices // QUAD
    chunks = kv_width // 2 // HD // QUAD
    back_layers = WINDOW // (QUAD * length)
    rows = seqs * length

    me = lax.axis_index("ctx")
    core = lax.axis_index("dp")
    r, layer = me % QUAD, me // QUAD

    def in_quad(block, m):
        return lax.ppermute(block, "ctx", [(i, i ^ m) for i in range(devices)])

    def other_core(block):
        return lax.ppermute(block, "dp", [(0, 1), (1, 0)])

    def layer_up(block):
        return lax.ppermute(block, "ctx", [(i, i + QUAD) for i in range(devices - QUAD)])

    ring = list(range(1, layers_total, 2))
    ring = [0] + ring + [i for i in range(layers_total - 1, 0, -1) if i % 2 == 0]
    place = {at: n for n, at in enumerate(ring)}
    ring_route = [
        (ring[n] * QUAD + q, ring[(n + 1) % layers_total] * QUAD + q)
        for n in range(layers_total)
        for q in range(QUAD)
    ]
    in_ring = shard_rows % 16 == 0 and layers_total <= 4
    if in_ring:
        origin = [
            [ring[(place[at] - k) % layers_total] for k in range(layers_total)]
            for at in range(layers_total)
        ]
        offsets = jnp.array(origin, dtype=jnp.int32)[layer]
    else:
        offsets = jnp.zeros((1,), jnp.int32)
    sc = jnp.concatenate([jnp.stack([r, core, layer]).astype(jnp.int32), offsets])

    w = kv_weight.reshape(shard_rows, 2, QUAD, chunks, HD)
    own_side = lax.dynamic_index_in_dim(w, core, 1, keepdims=False)
    other_side = lax.dynamic_index_in_dim(w, 1 - core, 1, keepdims=False)
    weights = []
    for a in range(chunks):
        own = own_side[:, :, a].reshape(shard_rows, QUAD * HD)
        if in_ring:
            pieces = [own, other_side[:, :, a].reshape(shard_rows, QUAD * HD)]
            for _ in range(layers_total - 1):
                own = lax.ppermute(own, "ctx", ring_route)
                pieces += [own, other_core(own)]
        else:
            lines = [[i * QUAD + q for i in range(layers_total)] for q in range(QUAD)]
            own = lax.all_gather(own, "ctx", axis=0, tiled=True, axis_index_groups=lines)
            pieces = [own, other_core(own)]
        weights.append(pieces)

    x = norm_slices(sc, hidden.reshape(rows, model_width), input_gain, shard_rows)
    x = [x[0]] + [in_quad(x[m], m) for m in range(1, QUAD)]

    slot_start = (layer * QUAD + (r ^ jnp.arange(QUAD, dtype=jnp.int32))) * length
    positions = (slot_start[:, None] + jnp.arange(length, dtype=jnp.int32)).reshape(-1)
    cos, sin = rotary_tables(positions, HD)
    cos, sin = cos.reshape(QUAD, length, HD), sin.reshape(QUAD, length, HD)

    q = query_slots(sc, queries.reshape(rows, -1), query_gain, cos[0], sin[0], seqs)
    q = [q[0]] + [in_quad(q[m], m) for m in range(1, QUAD)]

    outs = []
    for a in range(chunks):
        parts = project(sc, x, weights[a])
        parts = [parts[0]] + [in_quad(parts[m], m) for m in range(1, QUAD)]
        kvs = [reduce_parts(parts, key_gain, cos, sin, seqs)]
        for _ in range(back_layers):
            kvs.append(layer_up(kvs[-1]))
        o = attend(sc, q, kvs, a, chunks, seqs)
        outs.append([o[0]] + [in_quad(o[m], m) for m in range(1, QUAD)])
    slots = [outs[a][m] for m in range(QUAD) for a in range(chunks)]
    return assemble(sc, slots, chunks).reshape(seqs, length, -1)


def solution(mesh):
    return jax.shard_map(
        body,
        mesh=mesh,
        in_specs=(P("dp", "ctx", None), P("dp", "ctx", None), P(), P("ctx", None), P(), P()),
        out_specs=P("dp", "ctx", None),
        check_vma=False,
    )
```

```python
import functools

import jax
import jax.numpy as jnp
from jax import lax
from jax.experimental import pallas as pl
from jax.experimental.pallas import tpu as pltpu
from jax.sharding import PartitionSpec as P

HD = 128
WINDOW = 1024
QUAD = 4

attn_scalar = 168.0
norm_eps = 1e-06
F32 = jnp.float32
BF16 = jnp.bfloat16
MIB = 1 << 20


def params(mib, grid_dims=0):
    sem = ("arbitrary",) * grid_dims if grid_dims else None
    return pltpu.CompilerParams(vmem_limit_bytes=mib * MIB, dimension_semantics=sem)


COST = pl.CostEstimate(flops=0, bytes_accessed=0, transcendentals=0)
VMEM = pl.BlockSpec(memory_space=pltpu.VMEM)


def place_in_quad():
    return lax.axis_index("ctx") % QUAD


def rotary_tables(positions, head_width):
    half_width = head_width // 2
    exponent = 2.0 * jnp.arange(half_width, dtype=F32) / head_width
    inverse = jnp.power(10000.0, -exponent)
    angles = positions.astype(F32)[:, None] * inverse[None, :]
    cos, sin = jnp.cos(angles), jnp.sin(angles)
    return jnp.concatenate([cos, cos], axis=1), jnp.concatenate([-sin, sin], axis=1)


def norm_rotate(u, gain, cos, sin):
    scaled = u * lax.rsqrt(jnp.mean(u * u, axis=-1, keepdims=True) + norm_eps) * gain
    return scaled * cos + pltpu.roll(scaled, HD // 2, 1) * sin


def cut_kernel(chunks, side, w_ref, *outs):
    half = w_ref.shape[1] // 2
    at = (lax.axis_index("dp") ^ side) * half
    for a in range(chunks):
        for q in range(QUAD):
            column = pl.multiple_of(at + (q * chunks + a) * HD, HD)
            outs[a][:, q * HD : (q + 1) * HD] = w_ref[:, pl.ds(column, HD)]


def cut_weights(w, chunks, side):
    out = jax.ShapeDtypeStruct((w.shape[0], QUAD * HD), BF16)
    return pl.pallas_call(
        functools.partial(cut_kernel, chunks, side),
        in_specs=[VMEM],
        out_specs=[VMEM] * chunks,
        out_shape=[out] * chunks,
        cost_estimate=COST,
        compiler_params=params(16),
        name="cut_weights",
    )(w)


def norm_kernel(slices, width, x_ref, g_ref, *refs):
    outs, scratch = refs[:QUAD], refs[QUAD]
    seqs, step, total = x_ref.shape
    squares = jnp.zeros((seqs * step, HD), F32)
    for j in range(total // HD):
        x = x_ref[:, :, j * HD : (j + 1) * HD].astype(F32).reshape(seqs * step, HD)
        squares = squares + x * x
    mean = jnp.sum(squares, axis=-1, keepdims=True) * (1.0 / total)
    scale = lax.rsqrt(mean + norm_eps).reshape(seqs, step, 1)
    for i in range(slices):
        at = (i // QUAD) * width
        columns = slice(i * width, (i + 1) * width)
        y = x_ref[:, :, columns].astype(F32) * scale * g_ref[:, columns]
        scratch[i % QUAD, :, :, at : at + width] = y.astype(BF16)
    part = width * (slices // QUAD)
    full, rest = part // HD, part % HD
    r = place_in_quad()
    for m in range(QUAD):
        for s in range(seqs):
            for j in range(full):
                outs[m][j * seqs + s] = scratch[r ^ m, s, :, j * HD : (j + 1) * HD]
            if rest:
                outs[m][full * seqs, :, s * rest : (s + 1) * rest] = scratch[
                    r ^ m, s, :, full * HD :
                ]


def norm_slices(x, gain, shard_rows):
    seqs, length, width = x.shape
    part = width // QUAD
    blocks = part // HD * seqs + (1 if part % HD else 0)
    step = length // 4
    return pl.pallas_call(
        functools.partial(norm_kernel, width // shard_rows, shard_rows),
        grid=(4,),
        in_specs=[
            pl.BlockSpec((seqs, step, width), lambda i: (0, i, 0)),
            pl.BlockSpec((1, width), lambda i: (0, 0)),
        ],
        out_specs=[pl.BlockSpec((blocks, step, HD), lambda i: (0, i, 0))] * QUAD,
        out_shape=[jax.ShapeDtypeStruct((blocks, length, HD), BF16)] * QUAD,
        scratch_shapes=[pltpu.VMEM((QUAD, seqs, step, part), BF16)],
        cost_estimate=COST,
        compiler_params=params(32, 1),
        name="norm_slices",
    )(x, gain.reshape(1, width))


def query_kernel(seqs, q_ref, g_ref, cos_ref, sin_ref, *outs):
    width = outs[0].shape[1]
    length = cos_ref.shape[0]
    for m in range(QUAD):
        at = pl.multiple_of((place_in_quad() ^ m) * width, width)
        for s in range(seqs):
            for h in range(width // HD):
                u = q_ref[pl.ds(s * length, length), pl.ds(at + h * HD, HD)].astype(F32)
                y = norm_rotate(u, g_ref[...], cos_ref[...], sin_ref[...])
                y = y * attn_scalar ** (-0.5)
                outs[m][s * length : (s + 1) * length, h * HD : (h + 1) * HD] = y.astype(BF16)


def query_slots(q, gain, cos, sin, seqs):
    rows, width = q.shape
    return pl.pallas_call(
        functools.partial(query_kernel, seqs),
        in_specs=[VMEM] * 4,
        out_specs=[VMEM] * QUAD,
        out_shape=[jax.ShapeDtypeStruct((rows, width // QUAD), BF16)] * QUAD,
        cost_estimate=COST,
        compiler_params=params(16),
        name="query_slots",
    )(q, gain.reshape(1, HD), cos, sin)


def project_kernel(pieces, seqs, origin, *refs):
    xs, refs = refs[:QUAD], refs[QUAD:]
    own, other, refs = refs[:pieces], refs[pieces : pieces + 2], refs[pieces + 2 :]
    outs, refs = refs[: QUAD * seqs], refs[QUAD * seqs :]
    x_scr, w_scr = refs
    rows = own[0].shape[0]
    length = xs[0].shape[1]
    depth = w_scr.shape[2]
    full, rest = depth // HD, depth % HD
    core, r = lax.axis_index("dp"), place_in_quad()
    layer = lax.axis_index("ctx") // QUAD
    for k in range(pieces):
        from_layer = 0
        if pieces > 1:
            for n in range(pieces):
                from_layer = jnp.where(layer == n, origin[n][k], from_layer)
        at = pl.multiple_of(from_layer * rows, 16)
        theirs = other[0] if k == 0 else other[1].at[(k - 1) * rows : k * rows]
        for side, block in enumerate((own[k], theirs)):
            for q in range(QUAD):
                w_scr[q, core ^ side, pl.ds(at, rows), :] = block[:, q * HD : (q + 1) * HD]
    for s in range(seqs):
        for d in range(QUAD):
            at = slice(d * length, (d + 1) * length)
            for j in range(full):
                x_scr[s, at, j * HD : (j + 1) * HD] = xs[d][j * seqs + s]
            if rest:
                x_scr[s, at, full * HD :] = xs[d][full * seqs, :, s * rest : (s + 1) * rest]
    for s in range(seqs):
        for m in range(QUAD):
            q = r ^ m
            w = jnp.concatenate([w_scr[q, 0], w_scr[q, 1]], axis=1)
            y = jnp.dot(x_scr[s], w, preferred_element_type=F32)
            out = outs[s * QUAD + m]
            for d in range(QUAD):
                out[m ^ d] = y[d * length : (d + 1) * length].astype(out.dtype)


def project(xs, ws, seqs, depth, origin):
    length = xs[0].shape[1]
    pieces = len(ws) - 2
    shape = (QUAD, length, 2 * HD)
    shapes = [jax.ShapeDtypeStruct(shape, F32)]
    shapes += [jax.ShapeDtypeStruct(shape, BF16)] * (QUAD - 1)
    return pl.pallas_call(
        functools.partial(project_kernel, pieces, seqs, origin),
        in_specs=[VMEM] * (QUAD + len(ws)),
        out_specs=[VMEM] * (QUAD * seqs),
        out_shape=shapes * seqs,
        scratch_shapes=[
            pltpu.VMEM((seqs, QUAD * length, depth), BF16),
            pltpu.VMEM((QUAD, 2, depth, HD), BF16),
        ],
        cost_estimate=COST,
        compiler_params=params(32),
        name="project",
    )(*xs, *ws)


def reduce_kernel(*refs):
    parts, refs = refs[:QUAD], refs[QUAD:]
    g_ref, cos_ref, sin_ref, out_ref = refs
    for e in range(QUAD):
        total = parts[0][e]
        for part in parts[1:]:
            total = total + part[e].astype(F32)
        key = norm_rotate(total[:, :HD], g_ref[...], cos_ref[e], sin_ref[e])
        out_ref[e, :, :HD] = key.astype(BF16)
        out_ref[e, :, HD:] = total[:, HD:].astype(BF16)


def reduce_parts(parts, gain, cos, sin):
    return pl.pallas_call(
        reduce_kernel,
        in_specs=[VMEM] * (QUAD + 3),
        out_specs=VMEM,
        out_shape=jax.ShapeDtypeStruct(parts[0].shape, BF16),
        cost_estimate=COST,
        compiler_params=params(16),
        name="reduce_parts",
    )(*parts, gain.reshape(1, HD), cos, sin)


def attend_kernel(layers, seqs, *refs):
    qs, refs = refs[:QUAD], refs[QUAD:]
    kvs, refs = refs[: layers * seqs], refs[layers * seqs :]
    outs, refs = refs[:QUAD], refs[QUAD:]
    q_scr, k_scr, v_scr, o_scr = refs
    r, layer = place_in_quad(), lax.axis_index("ctx") // QUAD
    length = kvs[0].shape[1]
    heads = qs[0].shape[1] // HD
    span = QUAD * length
    shape = (heads * length, length)
    row = lax.broadcasted_iota(jnp.int32, (heads, length, length), 1).reshape(shape)
    column = lax.broadcasted_iota(jnp.int32, shape, 1)

    def load(s):
        for m in range(QUAD):
            for h in range(heads):
                q_scr[s, r ^ m, h * length : (h + 1) * length] = qs[m][
                    s * length : (s + 1) * length, h * HD : (h + 1) * HD
                ]
        for back in range(layers):
            for j in range(QUAD):
                at = (layers - 1 - back) * span + j * length
                kv = kvs[s * layers + back][r ^ j]
                k_scr[s, at : at + length] = kv[:, :HD]
                v_scr[s, at : at + length] = kv[:, HD:]

    def attend(back, s):
        for i in range(QUAD):
            stop = (layers - 1) * span + (i + 1) * length
            start = (layers - 1 - back) * span
            windowed = stop - length - WINDOW >= start
            if windowed:
                start = stop - length - WINDOW
            scores = lax.dot_general(
                q_scr[s, i],
                k_scr[s, start:stop],
                (((1,), (1,)), ((), ())),
                preferred_element_type=F32,
            )
            weights = jnp.exp(scores)
            blocks = [weights[:, :-length], jnp.where(column <= row, weights[:, -length:], 0.0)]
            if windowed:
                blocks[0] = jnp.concatenate(
                    [jnp.where(column > row, weights[:, :length], 0.0), blocks[0][:, length:]], axis=1
                )
            if blocks[0].shape[1] == 0:
                blocks = blocks[1:]
            weights = jnp.concatenate(blocks, axis=1)
            total = jnp.sum(weights, axis=-1, keepdims=True)
            out = jnp.dot(weights.astype(BF16), v_scr[s, start:stop], preferred_element_type=F32)
            out = (out / total).astype(BF16)
            for h in range(heads):
                o_scr[i, s * length : (s + 1) * length, h * HD : (h + 1) * HD] = out[
                    h * length : (h + 1) * length
                ]

    for s in range(seqs):
        load(s)
    for back in range(layers):
        here = layer == back if back < layers - 1 else layer >= back

        @pl.when(here)
        def _():
            for s in range(seqs):
                attend(back, s)

    for m in range(QUAD):
        outs[m][...] = o_scr[r ^ m]


def attend(qs, kvs, chunk, chunks, first):
    length = kvs[0][0].shape[1]
    width = qs[0].shape[1] // chunks
    seqs, layers = len(kvs), len(kvs[0])
    rows = seqs * length
    heads = width // HD
    place = first // seqs
    return pl.pallas_call(
        functools.partial(attend_kernel, layers, seqs),
        grid=(1,),
        in_specs=[pl.BlockSpec((rows, width), lambda i: (place, chunk))] * QUAD
        + [pl.BlockSpec((QUAD, length, 2 * HD), lambda i: (0, 0, 0))] * (layers * seqs),
        out_specs=[pl.BlockSpec((rows, width), lambda i: (0, 0))] * QUAD,
        out_shape=[jax.ShapeDtypeStruct((rows, width), BF16)] * QUAD,
        scratch_shapes=[
            pltpu.VMEM((seqs, QUAD, heads * length, HD), BF16),
            pltpu.VMEM((seqs, layers * QUAD * length, HD), BF16),
            pltpu.VMEM((seqs, layers * QUAD * length, HD), BF16),
            pltpu.VMEM((QUAD, rows, width), BF16),
        ],
        cost_estimate=COST,
        compiler_params=params(24, 1),
        name="attend",
    )(*qs, *[block for kv in kvs for block in kv])


def assemble_kernel(chunks, places, *refs):
    out, r = refs[-1], place_in_quad()
    for n, (a, s) in enumerate(places):
        for m in range(QUAD):
            block = refs[n * QUAD + m]
            rows, width = block.shape
            at = pl.multiple_of(((r ^ m) * chunks + a) * width, width)
            out[s : s + rows, pl.ds(at, width)] = block[...]


def assemble(slots, chunks, seqs, length):
    places, a, s = [], 0, 0
    for group in slots:
        places.append((a, s))
        s += group[0].shape[0]
        if s == seqs * length:
            a, s = a + 1, 0
    width = slots[0][0].shape[1]
    slots = [block for group in slots for block in group]
    return pl.pallas_call(
        functools.partial(assemble_kernel, chunks, places),
        in_specs=[VMEM] * len(slots),
        out_specs=VMEM,
        out_shape=jax.ShapeDtypeStruct((seqs * length, QUAD * chunks * width), BF16),
        cost_estimate=COST,
        compiler_params=params(16),
        name="assemble",
    )(*slots)


def body(hidden, queries, input_gain, kv_weight, query_gain, key_gain):
    seqs, length, model_width = hidden.shape
    shard_rows, kv_width = kv_weight.shape
    devices = lax.axis_size("ctx")
    layers_total = devices // QUAD
    chunks = kv_width // 2 // HD // QUAD
    back_layers = WINDOW // (QUAD * length)
    rows = seqs * length

    me = lax.axis_index("ctx")
    r, layer = me % QUAD, me // QUAD

    def in_quad(block, m):
        return lax.ppermute(block, "ctx", [(i, i ^ m) for i in range(devices)])

    def other_core(block):
        return lax.ppermute(block, "dp", [(0, 1), (1, 0)])

    def layer_up(block):
        return lax.ppermute(block, "ctx", [(i, i + QUAD) for i in range(devices - QUAD)])

    ring = list(range(1, layers_total, 2))
    ring = [0] + ring + [i for i in range(layers_total - 1, 0, -1) if i % 2 == 0]
    place = {at: n for n, at in enumerate(ring)}
    ring_route = [
        (ring[n] * QUAD + q, ring[(n + 1) % layers_total] * QUAD + q)
        for n in range(layers_total)
        for q in range(QUAD)
    ]
    in_ring = shard_rows % 16 == 0 and layers_total <= 4
    origin = [
        [ring[(place[at] - k) % layers_total] for k in range(layers_total)]
        for at in range(layers_total)
    ]

    def exchange(slots):
        return [slots[0]] + [in_quad(slots[m], m) for m in range(1, QUAD)]

    def together(values):
        return list(lax.optimization_barrier(values))

    cut = cut_weights(kv_weight, chunks, 0)

    if in_ring:
        rings = [[own] for own in cut]
        for _ in range(layers_total - 1):
            for pieces in rings:
                pieces.append(lax.ppermute(pieces[-1], "ctx", ring_route))
    else:
        lines = [[i * QUAD + q for i in range(layers_total)] for q in range(QUAD)]
        rings = [
            [lax.all_gather(own, "ctx", axis=0, tiled=True, axis_index_groups=lines)]
            for own in cut
        ]

    def both_sides(a):
        if in_ring:
            return rings[a] + [cut_other[a], other_core(jnp.concatenate(rings[a][1:], axis=0))]
        other = other_core(rings[a][0])
        return rings[a] + [other, other]

    x = norm_slices(hidden, input_gain, shard_rows)

    slots = jnp.arange(QUAD, dtype=jnp.int32)
    own, slots, queries, w = together((x[0], slots, queries, kv_weight))
    cut_other = cut_weights(w, chunks, 1)
    x = [own] + exchange(x)[1:]
    slot_start = (layer * QUAD + (r ^ slots)) * length
    positions = (slot_start[:, None] + jnp.arange(length, dtype=jnp.int32)).reshape(-1)
    cos, sin = rotary_tables(positions, HD)
    cos, sin = cos.reshape(QUAD, length, HD), sin.reshape(QUAD, length, HD)
    q = query_slots(queries.reshape(rows, -1), query_gain, cos[0], sin[0], seqs)
    early = [pieces[: max(1, len(pieces) - 1)] for pieces in rings[1:]]
    x, rings[0], early, cos, sin, q = together((x, rings[0], early, cos, sin, q))
    q = exchange(q)

    def project_chunk(weights):
        made = list(project(x, weights, seqs, model_width // QUAD, origin))
        return [made[s * QUAD : (s + 1) * QUAD] for s in range(seqs)]

    total = chunks * seqs
    parts = project_chunk(both_sides(0))
    parts, q, rings[1:] = together((parts, q, rings[1:]))
    sent = [exchange(part) for part in parts]
    for a in range(1, chunks):
        parts += project_chunk(both_sides(a))
    sent[0], parts[seqs:] = together((sent[0], parts[seqs:]))

    kvs, outs = [], []

    def up(n):
        kvs[n].append(layer_up(kvs[n][-1]))

    for n in range(total):
        if n >= 1:
            sent[n], kvs[n - 1] = together((sent[n], kvs[n - 1]))
            for _ in range(back_layers - 1):
                up(n - 1)
        if n >= 2:
            sent[n], kvs[n - 2] = together((sent[n], kvs[n - 2]))
        if n >= seqs + 1 and n % seqs == 1:
            out = attend(q, kvs[n - 1 - seqs : n - 1], n // seqs - 1, chunks, 0)
            if n < total - 1:
                sent[n], out = together((sent[n], out))
            outs.append(exchange(out))
        kv = reduce_parts(sent[n], key_gain, cos, sin)
        if n + seqs < total:
            parts[n + seqs], kv = together((parts[n + seqs], kv))
            sent.append(exchange(parts[n + seqs]))
        kvs.append([kv, layer_up(kv)])
    kvs[-1][1], outs[-1] = together((kvs[-1][1], outs[-1]))
    for _ in range(back_layers - 1):
        up(total - 1)
    for n in range(total - seqs, total):
        if n == total - 2:
            kvs[n], kvs[n + 1][1] = together((kvs[n], kvs[n + 1][1]))
        outs.append(exchange(attend(q, [kvs[n]], n // seqs, chunks, n % seqs)))
    return assemble(outs, chunks, seqs, length).reshape(seqs, length, -1)


def solution(mesh):
    return jax.shard_map(
        body,
        mesh=mesh,
        in_specs=(P("dp", "ctx", None), P("dp", "ctx", None), P(), P("ctx", None), P(), P()),
        out_specs=P("dp", "ctx", None),
        check_vma=False,
    )
```

```python
import functools

import jax
import jax.numpy as jnp
from jax import lax
from jax.experimental import pallas as pl
from jax.experimental.pallas import tpu as pltpu
from jax.sharding import PartitionSpec as P

HD = 128
WINDOW = 1024
QUAD = 4

attn_scalar = 168.0
norm_eps = 1e-06
F32 = jnp.float32
BF16 = jnp.bfloat16
MIB = 1 << 20


def params(mib, grid_dims=0):
    sem = ("arbitrary",) * grid_dims if grid_dims else None
    return pltpu.CompilerParams(vmem_limit_bytes=mib * MIB, dimension_semantics=sem)


COST = pl.CostEstimate(flops=0, bytes_accessed=0, transcendentals=0)
VMEM = pl.BlockSpec(memory_space=pltpu.VMEM)


def place_in_quad():
    return lax.axis_index("ctx") % QUAD


def rotary_tables(positions, head_width):
    half_width = head_width // 2
    exponent = 2.0 * jnp.arange(half_width, dtype=F32) / head_width
    inverse = jnp.power(10000.0, -exponent)
    angles = positions.astype(F32)[:, None] * inverse[None, :]
    cos, sin = jnp.cos(angles), jnp.sin(angles)
    return jnp.concatenate([cos, cos], axis=1), jnp.concatenate([-sin, sin], axis=1)


def norm_rotate(u, gain, cos, sin):
    scaled = u * lax.rsqrt(jnp.mean(u * u, axis=-1, keepdims=True) + norm_eps) * gain
    return scaled * cos + pltpu.roll(scaled, HD // 2, 1) * sin


def cut_kernel(chunks, side, w_ref, *outs):
    half = w_ref.shape[1] // 2
    at = (lax.axis_index("dp") ^ side) * half
    for a in range(chunks):
        for q in range(QUAD):
            column = pl.multiple_of(at + (q * chunks + a) * HD, HD)
            outs[a][:, q * HD : (q + 1) * HD] = w_ref[:, pl.ds(column, HD)]


def cut_weights(w, chunks, side):
    out = jax.ShapeDtypeStruct((w.shape[0], QUAD * HD), BF16)
    return pl.pallas_call(
        functools.partial(cut_kernel, chunks, side),
        in_specs=[VMEM],
        out_specs=[VMEM] * chunks,
        out_shape=[out] * chunks,
        cost_estimate=COST,
        compiler_params=params(16),
        name="cut_weights",
    )(w)


def norm_kernel(slices, width, x_ref, g_ref, *refs):
    outs, scratch = refs[:QUAD], refs[QUAD]
    seqs, step, total = x_ref.shape
    squares = jnp.zeros((seqs * step, HD), F32)
    for j in range(total // HD):
        x = x_ref[:, :, j * HD : (j + 1) * HD].astype(F32).reshape(seqs * step, HD)
        squares = squares + x * x
    mean = jnp.sum(squares, axis=-1, keepdims=True) * (1.0 / total)
    scale = lax.rsqrt(mean + norm_eps).reshape(seqs, step, 1)
    for i in range(slices):
        at = (i // QUAD) * width
        columns = slice(i * width, (i + 1) * width)
        y = x_ref[:, :, columns].astype(F32) * scale * g_ref[:, columns]
        scratch[i % QUAD, :, :, at : at + width] = y.astype(BF16)
    part = width * (slices // QUAD)
    full, rest = part // HD, part % HD
    r = place_in_quad()
    for m in range(QUAD):
        for s in range(seqs):
            for j in range(full):
                outs[m][j * seqs + s] = scratch[r ^ m, s, :, j * HD : (j + 1) * HD]
            if rest:
                outs[m][full * seqs, :, s * rest : (s + 1) * rest] = scratch[
                    r ^ m, s, :, full * HD :
                ]


def norm_slices(x, gain, shard_rows):
    seqs, length, width = x.shape
    part = width // QUAD
    blocks = part // HD * seqs + (1 if part % HD else 0)
    step = length // 4
    return pl.pallas_call(
        functools.partial(norm_kernel, width // shard_rows, shard_rows),
        grid=(4,),
        in_specs=[
            pl.BlockSpec((seqs, step, width), lambda i: (0, i, 0)),
            pl.BlockSpec((1, width), lambda i: (0, 0)),
        ],
        out_specs=[pl.BlockSpec((blocks, step, HD), lambda i: (0, i, 0))] * QUAD,
        out_shape=[jax.ShapeDtypeStruct((blocks, length, HD), BF16)] * QUAD,
        scratch_shapes=[pltpu.VMEM((QUAD, seqs, step, part), BF16)],
        cost_estimate=COST,
        compiler_params=params(32, 1),
        name="norm_slices",
    )(x, gain.reshape(1, width))


def query_kernel(seqs, q_ref, g_ref, cos_ref, sin_ref, *outs):
    width = outs[0].shape[1]
    length = cos_ref.shape[0]
    for m in range(QUAD):
        at = pl.multiple_of((place_in_quad() ^ m) * width, width)
        for s in range(seqs):
            for h in range(width // HD):
                u = q_ref[pl.ds(s * length, length), pl.ds(at + h * HD, HD)].astype(F32)
                y = norm_rotate(u, g_ref[...], cos_ref[...], sin_ref[...])
                y = y * attn_scalar ** (-0.5)
                outs[m][s * length : (s + 1) * length, h * HD : (h + 1) * HD] = y.astype(BF16)


def query_slots(q, gain, cos, sin, seqs):
    rows, width = q.shape
    return pl.pallas_call(
        functools.partial(query_kernel, seqs),
        in_specs=[VMEM] * 4,
        out_specs=[VMEM] * QUAD,
        out_shape=[jax.ShapeDtypeStruct((rows, width // QUAD), BF16)] * QUAD,
        cost_estimate=COST,
        compiler_params=params(16),
        name="query_slots",
    )(q, gain.reshape(1, HD), cos, sin)


def project_kernel(pieces, seqs, seq, origin, *refs):
    xs, refs = refs[:QUAD], refs[QUAD:]
    own, other, refs = refs[:pieces], refs[pieces : pieces + 2], refs[pieces + 2 :]
    outs, refs = refs[:QUAD], refs[QUAD:]
    x_scr, w_scr = refs
    rows = own[0].shape[0]
    length = xs[0].shape[1]
    depth = w_scr.shape[2]
    full, rest = depth // HD, depth % HD
    core, r = lax.axis_index("dp"), place_in_quad()
    layer = lax.axis_index("ctx") // QUAD
    for k in range(pieces):
        from_layer = 0
        if pieces > 1:
            for n in range(pieces):
                from_layer = jnp.where(layer == n, origin[n][k], from_layer)
        at = pl.multiple_of(from_layer * rows, 16)
        theirs = other[0] if k == 0 else other[1].at[(k - 1) * rows : k * rows]
        for side, block in enumerate((own[k], theirs)):
            for q in range(QUAD):
                w_scr[q, core ^ side, pl.ds(at, rows), :] = block[:, q * HD : (q + 1) * HD]
    for d in range(QUAD):
        at = slice(d * length, (d + 1) * length)
        for j in range(full):
            x_scr[at, j * HD : (j + 1) * HD] = xs[d][j * seqs + seq]
        if rest:
            x_scr[at, full * HD :] = xs[d][full * seqs, :, seq * rest : (seq + 1) * rest]
    for m in range(QUAD):
        q = r ^ m
        w = jnp.concatenate([w_scr[q, 0], w_scr[q, 1]], axis=1)
        y = jnp.dot(x_scr[...], w, preferred_element_type=F32)
        for d in range(QUAD):
            outs[m][m ^ d] = y[d * length : (d + 1) * length].astype(outs[m].dtype)


def project(xs, ws, seqs, seq, depth, origin):
    length = xs[0].shape[1]
    pieces = len(ws) - 2
    shape = (QUAD, length, 2 * HD)
    shapes = [jax.ShapeDtypeStruct(shape, F32)]
    shapes += [jax.ShapeDtypeStruct(shape, BF16)] * (QUAD - 1)
    return pl.pallas_call(
        functools.partial(project_kernel, pieces, seqs, seq, origin),
        in_specs=[VMEM] * (QUAD + len(ws)),
        out_specs=[VMEM] * QUAD,
        out_shape=shapes,
        scratch_shapes=[
            pltpu.VMEM((QUAD * length, depth), BF16),
            pltpu.VMEM((QUAD, 2, depth, HD), BF16),
        ],
        cost_estimate=COST,
        compiler_params=params(32),
        name="project",
    )(*xs, *ws)


def reduce_kernel(*refs):
    parts, refs = refs[:QUAD], refs[QUAD:]
    g_ref, cos_ref, sin_ref, out_ref = refs
    for e in range(QUAD):
        total = parts[0][e]
        for part in parts[1:]:
            total = total + part[e].astype(F32)
        key = norm_rotate(total[:, :HD], g_ref[...], cos_ref[e], sin_ref[e])
        out_ref[e, :, :HD] = key.astype(BF16)
        out_ref[e, :, HD:] = total[:, HD:].astype(BF16)


def reduce_parts(parts, gain, cos, sin):
    return pl.pallas_call(
        reduce_kernel,
        in_specs=[VMEM] * (QUAD + 3),
        out_specs=VMEM,
        out_shape=jax.ShapeDtypeStruct(parts[0].shape, BF16),
        cost_estimate=COST,
        compiler_params=params(16),
        name="reduce_parts",
    )(*parts, gain.reshape(1, HD), cos, sin)


def attend_kernel(layers, seqs, *refs):
    qs, refs = refs[:QUAD], refs[QUAD:]
    kvs, refs = refs[: layers * seqs], refs[layers * seqs :]
    outs, refs = refs[:QUAD], refs[QUAD:]
    q_scr, k_scr, v_scr, o_scr = refs
    r, layer = place_in_quad(), lax.axis_index("ctx") // QUAD
    length = kvs[0].shape[1]
    heads = qs[0].shape[1] // HD
    span = QUAD * length
    shape = (heads * length, length)
    row = lax.broadcasted_iota(jnp.int32, (heads, length, length), 1).reshape(shape)
    column = lax.broadcasted_iota(jnp.int32, shape, 1)

    def load(s):
        for m in range(QUAD):
            for h in range(heads):
                q_scr[s, r ^ m, h * length : (h + 1) * length] = qs[m][
                    s * length : (s + 1) * length, h * HD : (h + 1) * HD
                ]
        for back in range(layers):
            for j in range(QUAD):
                at = (layers - 1 - back) * span + j * length
                kv = kvs[s * layers + back][r ^ j]
                k_scr[s, at : at + length] = kv[:, :HD]
                v_scr[s, at : at + length] = kv[:, HD:]

    def attend(back, s):
        for i in range(QUAD):
            stop = (layers - 1) * span + (i + 1) * length
            start = (layers - 1 - back) * span
            windowed = stop - length - WINDOW >= start
            if windowed:
                start = stop - length - WINDOW
            scores = lax.dot_general(
                q_scr[s, i],
                k_scr[s, start:stop],
                (((1,), (1,)), ((), ())),
                preferred_element_type=F32,
            )
            weights = jnp.exp(scores)
            blocks = [weights[:, :-length], jnp.where(column <= row, weights[:, -length:], 0.0)]
            if windowed:
                blocks[0] = jnp.concatenate(
                    [jnp.where(column > row, weights[:, :length], 0.0), blocks[0][:, length:]], axis=1
                )
            if blocks[0].shape[1] == 0:
                blocks = blocks[1:]
            weights = jnp.concatenate(blocks, axis=1)
            total = jnp.sum(weights, axis=-1, keepdims=True)
            out = jnp.dot(weights.astype(BF16), v_scr[s, start:stop], preferred_element_type=F32)
            out = (out / total).astype(BF16)
            for h in range(heads):
                o_scr[i, s * length : (s + 1) * length, h * HD : (h + 1) * HD] = out[
                    h * length : (h + 1) * length
                ]

    for s in range(seqs):
        load(s)
    for back in range(layers):
        here = layer == back if back < layers - 1 else layer >= back

        @pl.when(here)
        def _():
            for s in range(seqs):
                attend(back, s)

    for m in range(QUAD):
        outs[m][...] = o_scr[r ^ m]


def attend(qs, kvs, chunk, chunks, first):
    length = kvs[0][0].shape[1]
    width = qs[0].shape[1] // chunks
    seqs, layers = len(kvs), len(kvs[0])
    rows = seqs * length
    heads = width // HD
    place = first // seqs
    return pl.pallas_call(
        functools.partial(attend_kernel, layers, seqs),
        grid=(1,),
        in_specs=[pl.BlockSpec((rows, width), lambda i: (place, chunk))] * QUAD
        + [pl.BlockSpec((QUAD, length, 2 * HD), lambda i: (0, 0, 0))] * (layers * seqs),
        out_specs=[pl.BlockSpec((rows, width), lambda i: (0, 0))] * QUAD,
        out_shape=[jax.ShapeDtypeStruct((rows, width), BF16)] * QUAD,
        scratch_shapes=[
            pltpu.VMEM((seqs, QUAD, heads * length, HD), BF16),
            pltpu.VMEM((seqs, layers * QUAD * length, HD), BF16),
            pltpu.VMEM((seqs, layers * QUAD * length, HD), BF16),
            pltpu.VMEM((QUAD, rows, width), BF16),
        ],
        cost_estimate=COST,
        compiler_params=params(24, 1),
        name="attend",
    )(*qs, *[block for kv in kvs for block in kv])


def assemble_kernel(chunks, places, *refs):
    out, r = refs[-1], place_in_quad()
    for n, (a, s) in enumerate(places):
        for m in range(QUAD):
            block = refs[n * QUAD + m]
            rows, width = block.shape
            at = pl.multiple_of(((r ^ m) * chunks + a) * width, width)
            out[s : s + rows, pl.ds(at, width)] = block[...]


def assemble(slots, chunks, seqs, length):
    places, a, s = [], 0, 0
    for group in slots:
        places.append((a, s))
        s += group[0].shape[0]
        if s == seqs * length:
            a, s = a + 1, 0
    width = slots[0][0].shape[1]
    slots = [block for group in slots for block in group]
    return pl.pallas_call(
        functools.partial(assemble_kernel, chunks, places),
        in_specs=[VMEM] * len(slots),
        out_specs=VMEM,
        out_shape=jax.ShapeDtypeStruct((seqs * length, QUAD * chunks * width), BF16),
        cost_estimate=COST,
        compiler_params=params(16),
        name="assemble",
    )(*slots)


def body(hidden, queries, input_gain, kv_weight, query_gain, key_gain):
    seqs, length, model_width = hidden.shape
    shard_rows, kv_width = kv_weight.shape
    devices = lax.axis_size("ctx")
    layers_total = devices // QUAD
    chunks = kv_width // 2 // HD // QUAD
    back_layers = WINDOW // (QUAD * length)
    rows = seqs * length

    me = lax.axis_index("ctx")
    r, layer = me % QUAD, me // QUAD

    def in_quad(block, m):
        return lax.ppermute(block, "ctx", [(i, i ^ m) for i in range(devices)])

    def other_core(block):
        return lax.ppermute(block, "dp", [(0, 1), (1, 0)])

    def layer_up(block):
        return lax.ppermute(block, "ctx", [(i, (i + QUAD) % devices) for i in range(devices)])

    ring = list(range(1, layers_total, 2))
    ring = [0] + ring + [i for i in range(layers_total - 1, 0, -1) if i % 2 == 0]
    place = {at: n for n, at in enumerate(ring)}
    ring_route = [
        (ring[n] * QUAD + q, ring[(n + 1) % layers_total] * QUAD + q)
        for n in range(layers_total)
        for q in range(QUAD)
    ]
    in_ring = shard_rows % 16 == 0 and layers_total <= 4
    origin = [
        [ring[(place[at] - k) % layers_total] for k in range(layers_total)]
        for at in range(layers_total)
    ]

    def exchange(slots):
        return [slots[0]] + [in_quad(slots[m], m) for m in range(1, QUAD)]

    def together(values):
        return list(lax.optimization_barrier(values))

    cut = cut_weights(kv_weight, chunks, 0)

    if in_ring:
        rings = [[own] for own in cut]
        for _ in range(layers_total - 1):
            for pieces in rings:
                pieces.append(lax.ppermute(pieces[-1], "ctx", ring_route))
    else:
        lines = [[i * QUAD + q for i in range(layers_total)] for q in range(QUAD)]
        rings = [
            [lax.all_gather(own, "ctx", axis=0, tiled=True, axis_index_groups=lines)]
            for own in cut
        ]

    def both_sides(a):
        if in_ring:
            return rings[a] + [cut_other[a], other_core(jnp.concatenate(rings[a][1:], axis=0))]
        other = other_core(rings[a][0])
        return rings[a] + [other, other]

    x = norm_slices(hidden, input_gain, shard_rows)

    slots = jnp.arange(QUAD, dtype=jnp.int32)
    own, slots, queries, w = together((x[0], slots, queries, kv_weight))
    cut_other = cut_weights(w, chunks, 1)
    x = [own] + exchange(x)[1:]
    slot_start = (layer * QUAD + (r ^ slots)) * length
    positions = (slot_start[:, None] + jnp.arange(length, dtype=jnp.int32)).reshape(-1)
    cos, sin = rotary_tables(positions, HD)
    cos, sin = cos.reshape(QUAD, length, HD), sin.reshape(QUAD, length, HD)
    q = query_slots(queries.reshape(rows, -1), query_gain, cos[0], sin[0], seqs)
    early = [pieces[: max(1, len(pieces) - 1)] for pieces in rings[1:]]
    x, rings[0], early, cos, sin, q = together((x, rings[0], early, cos, sin, q))
    q = exchange(q)

    def project_chunk(weights):
        return [
            list(project(x, weights, seqs, s, model_width // QUAD, origin)) for s in range(seqs)
        ]

    total = chunks * seqs
    parts = project_chunk(both_sides(0))
    sent = [exchange(part) for part in parts]
    for a in range(1, chunks):
        parts += project_chunk(both_sides(a))
    sent[0], parts[seqs:] = together((sent[0], parts[seqs:]))

    kvs, outs = [], []

    def up(n):
        kvs[n].append(layer_up(kvs[n][-1]))

    for n in range(total):
        if n >= 1:
            sent[n], kvs[n - 1] = together((sent[n], kvs[n - 1]))
            for _ in range(back_layers - 1):
                up(n - 1)
        if 2 <= n < total - 1:
            sent[n], kvs[n - 2] = together((sent[n], kvs[n - 2]))
        if n >= seqs + 1 and n % seqs == 1:
            out = attend(q, kvs[n - 1 - seqs : n - 1], n // seqs - 1, chunks, 0)
            if n < total - 1:
                sent[n], out = together((sent[n], out))
            outs.append(exchange(out))
        kv = reduce_parts(sent[n], key_gain, cos, sin)
        if n + seqs < total:
            parts[n + seqs], kv = together((parts[n + seqs], kv))
            sent.append(exchange(parts[n + seqs]))
        kvs.append([kv, layer_up(kv)])
    kvs[-1][1], kvs[-3] = together((kvs[-1][1], kvs[-3]))
    for _ in range(back_layers - 1):
        up(total - 1)
    for n in range(total - seqs, total):
        if n == total - 2:
            kvs[n], kvs[n + 1][1] = together((kvs[n], kvs[n + 1][1]))
        outs.append(exchange(attend(q, [kvs[n]], n // seqs, chunks, n % seqs)))
    return assemble(outs, chunks, seqs, length).reshape(seqs, length, -1)


def solution(mesh):
    return jax.shard_map(
        body,
        mesh=mesh,
        in_specs=(P("dp", "ctx", None), P("dp", "ctx", None), P(), P("ctx", None), P(), P()),
        out_specs=P("dp", "ctx", None),
        check_vma=False,
    )
```

```python
import functools

import jax
import jax.numpy as jnp
from jax import lax
from jax.experimental import pallas as pl
from jax.experimental.pallas import tpu as pltpu
from jax.sharding import PartitionSpec as P

HD = 128
WINDOW = 1024
QUAD = 4

attn_scalar = 168.0
norm_eps = 1e-06
F32 = jnp.float32
BF16 = jnp.bfloat16
MIB = 1 << 20


def params(mib, grid_dims=0):
    sem = ("arbitrary",) * grid_dims if grid_dims else None
    return pltpu.CompilerParams(vmem_limit_bytes=mib * MIB, dimension_semantics=sem)


COST = pl.CostEstimate(flops=0, bytes_accessed=0, transcendentals=0)
VMEM = pl.BlockSpec(memory_space=pltpu.VMEM)


def place_in_quad():
    return lax.axis_index("ctx") % QUAD


def rotary_tables(positions, head_width):
    half_width = head_width // 2
    exponent = 2.0 * jnp.arange(half_width, dtype=F32) / head_width
    inverse = jnp.power(10000.0, -exponent)
    angles = positions.astype(F32)[:, None] * inverse[None, :]
    cos, sin = jnp.cos(angles), jnp.sin(angles)
    return jnp.concatenate([cos, cos], axis=1), jnp.concatenate([-sin, sin], axis=1)


def norm_rotate(u, gain, cos, sin):
    scaled = u * lax.rsqrt(jnp.mean(u * u, axis=-1, keepdims=True) + norm_eps) * gain
    return scaled * cos + pltpu.roll(scaled, HD // 2, 1) * sin


def cut_kernel(chunks, side, w_ref, *outs):
    half = w_ref.shape[1] // 2
    at = (lax.axis_index("dp") ^ side) * half
    for a in range(chunks):
        for q in range(QUAD):
            column = pl.multiple_of(at + (q * chunks + a) * HD, HD)
            outs[a][:, q * HD : (q + 1) * HD] = w_ref[:, pl.ds(column, HD)]


def cut_weights(w, chunks, side):
    out = jax.ShapeDtypeStruct((w.shape[0], QUAD * HD), BF16)
    return pl.pallas_call(
        functools.partial(cut_kernel, chunks, side),
        in_specs=[VMEM],
        out_specs=[VMEM] * chunks,
        out_shape=[out] * chunks,
        cost_estimate=COST,
        compiler_params=params(16),
        name="cut_weights",
    )(w)


def norm_kernel(slices, width, x_ref, g_ref, *refs):
    outs, scratch, gain = refs[:QUAD], refs[QUAD], refs[QUAD + 1]
    seqs, step, total = x_ref.shape

    @pl.when(pl.program_id(0) == 0)
    def _():
        for j in range(total // HD):
            gain[:, j * HD : (j + 1) * HD] = g_ref[j : j + 1]

    squares = jnp.zeros((seqs * step, HD), F32)
    for j in range(total // HD):
        x = x_ref[:, :, j * HD : (j + 1) * HD].astype(F32).reshape(seqs * step, HD)
        squares = squares + x * x
    mean = jnp.sum(squares, axis=-1, keepdims=True) * (1.0 / total)
    scale = lax.rsqrt(mean + norm_eps).reshape(seqs, step, 1)
    for i in range(slices):
        at = (i // QUAD) * width
        columns = slice(i * width, (i + 1) * width)
        y = x_ref[:, :, columns].astype(F32) * scale * gain[:, columns]
        scratch[i % QUAD, :, :, at : at + width] = y.astype(BF16)
    part = width * (slices // QUAD)
    full, rest = part // HD, part % HD
    r = place_in_quad()
    for m in range(QUAD):
        for s in range(seqs):
            for j in range(full):
                outs[m][j * seqs + s] = scratch[r ^ m, s, :, j * HD : (j + 1) * HD]
            if rest:
                outs[m][full * seqs, :, s * rest : (s + 1) * rest] = scratch[
                    r ^ m, s, :, full * HD :
                ]


def norm_slices(x, gain, shard_rows):
    seqs, length, width = x.shape
    part = width // QUAD
    blocks = part // HD * seqs + (1 if part % HD else 0)
    step = length // 4
    return pl.pallas_call(
        functools.partial(norm_kernel, width // shard_rows, shard_rows),
        grid=(4,),
        in_specs=[
            pl.BlockSpec((seqs, step, width), lambda i: (0, i, 0)),
            pl.BlockSpec((width // HD, HD), lambda i: (0, 0)),
        ],
        out_specs=[pl.BlockSpec((blocks, step, HD), lambda i: (0, i, 0))] * QUAD,
        out_shape=[jax.ShapeDtypeStruct((blocks, length, HD), BF16)] * QUAD,
        scratch_shapes=[pltpu.VMEM((QUAD, seqs, step, part), BF16), pltpu.VMEM((1, width), F32)],
        cost_estimate=COST,
        compiler_params=params(60, 1),
        name="norm_slices",
    )(x, gain.reshape(width // HD, HD))


def query_kernel(seqs, q_ref, g_ref, cos_ref, sin_ref, *outs):
    width = outs[0].shape[1]
    length = cos_ref.shape[0]
    for m in range(QUAD):
        at = pl.multiple_of((place_in_quad() ^ m) * width, width)
        for s in range(seqs):
            for h in range(width // HD):
                u = q_ref[pl.ds(s * length, length), pl.ds(at + h * HD, HD)].astype(F32)
                y = norm_rotate(u, g_ref[...], cos_ref[...], sin_ref[...])
                y = y * attn_scalar ** (-0.5)
                outs[m][s * length : (s + 1) * length, h * HD : (h + 1) * HD] = y.astype(BF16)


def query_slots(q, gain, cos, sin, seqs):
    rows, width = q.shape
    return pl.pallas_call(
        functools.partial(query_kernel, seqs),
        in_specs=[VMEM] * 4,
        out_specs=[VMEM] * QUAD,
        out_shape=[jax.ShapeDtypeStruct((rows, width // QUAD), BF16)] * QUAD,
        cost_estimate=COST,
        compiler_params=params(16),
        name="query_slots",
    )(q, gain.reshape(1, HD), cos, sin)


def project_kernel(pieces, seqs, seq, origin, *refs):
    xs, refs = refs[:QUAD], refs[QUAD:]
    own, other, refs = refs[:pieces], refs[pieces : pieces + 2], refs[pieces + 2 :]
    outs, refs = refs[:QUAD], refs[QUAD:]
    x_scr, w_scr = refs
    rows = own[0].shape[0]
    length = xs[0].shape[1]
    depth = w_scr.shape[2]
    full, rest = depth // HD, depth % HD
    core, r = lax.axis_index("dp"), place_in_quad()
    layer = lax.axis_index("ctx") // QUAD
    for k in range(pieces):
        from_layer = 0
        if pieces > 1:
            for n in range(pieces):
                from_layer = jnp.where(layer == n, origin[n][k], from_layer)
        at = pl.multiple_of(from_layer * rows, 16)
        theirs = other[0] if k == 0 else other[1].at[(k - 1) * rows : k * rows]
        for side, block in enumerate((own[k], theirs)):
            for q in range(QUAD):
                w_scr[q, core ^ side, pl.ds(at, rows), :] = block[:, q * HD : (q + 1) * HD]
    for d in range(QUAD):
        at = slice(d * length, (d + 1) * length)
        for j in range(full):
            x_scr[at, j * HD : (j + 1) * HD] = xs[d][j * seqs + seq]
        if rest:
            x_scr[at, full * HD :] = xs[d][full * seqs, :, seq * rest : (seq + 1) * rest]
    for m in range(QUAD):
        q = r ^ m
        w = jnp.concatenate([w_scr[q, 0], w_scr[q, 1]], axis=1)
        y = jnp.dot(x_scr[...], w, preferred_element_type=F32)
        for d in range(QUAD):
            outs[m][m ^ d] = y[d * length : (d + 1) * length].astype(outs[m].dtype)


def project(xs, ws, seqs, seq, depth, origin):
    length = xs[0].shape[1]
    pieces = len(ws) - 2
    shape = (QUAD, length, 2 * HD)
    shapes = [jax.ShapeDtypeStruct(shape, F32)]
    shapes += [jax.ShapeDtypeStruct(shape, BF16)] * (QUAD - 1)
    return pl.pallas_call(
        functools.partial(project_kernel, pieces, seqs, seq, origin),
        in_specs=[VMEM] * (QUAD + len(ws)),
        out_specs=[VMEM] * QUAD,
        out_shape=shapes,
        scratch_shapes=[
            pltpu.VMEM((QUAD * length, depth), BF16),
            pltpu.VMEM((QUAD, 2, depth, HD), BF16),
        ],
        cost_estimate=COST,
        compiler_params=params(32),
        name="project",
    )(*xs, *ws)


def reduce_kernel(*refs):
    parts, refs = refs[:QUAD], refs[QUAD:]
    g_ref, cos_ref, sin_ref, out_ref = refs
    for e in range(QUAD):
        total = parts[0][e]
        for part in parts[1:]:
            total = total + part[e].astype(F32)
        key = norm_rotate(total[:, :HD], g_ref[...], cos_ref[e], sin_ref[e])
        out_ref[e, :, :HD] = key.astype(BF16)
        out_ref[e, :, HD:] = total[:, HD:].astype(BF16)


def reduce_parts(parts, gain, cos, sin):
    return pl.pallas_call(
        reduce_kernel,
        in_specs=[VMEM] * (QUAD + 3),
        out_specs=VMEM,
        out_shape=jax.ShapeDtypeStruct(parts[0].shape, BF16),
        cost_estimate=COST,
        compiler_params=params(16),
        name="reduce_parts",
    )(*parts, gain.reshape(1, HD), cos, sin)


def attend_kernel(layers, seqs, *refs):
    qs, refs = refs[:QUAD], refs[QUAD:]
    kvs, refs = refs[: layers * seqs], refs[layers * seqs :]
    outs, refs = refs[:QUAD], refs[QUAD:]
    q_scr, k_scr, v_scr, o_scr = refs
    r, layer = place_in_quad(), lax.axis_index("ctx") // QUAD
    length = kvs[0].shape[1]
    heads = qs[0].shape[1] // HD
    span = QUAD * length
    shape = (heads * length, length)
    row = lax.broadcasted_iota(jnp.int32, (heads, length, length), 1).reshape(shape)
    column = lax.broadcasted_iota(jnp.int32, shape, 1)

    def load(s):
        for m in range(QUAD):
            for h in range(heads):
                q_scr[s, r ^ m, h * length : (h + 1) * length] = qs[m][
                    s * length : (s + 1) * length, h * HD : (h + 1) * HD
                ]
        for back in range(layers):
            for j in range(QUAD):
                at = (layers - 1 - back) * span + j * length
                kv = kvs[s * layers + back][r ^ j]
                k_scr[s, at : at + length] = kv[:, :HD]
                v_scr[s, at : at + length] = kv[:, HD:]

    def attend(back, s):
        for i in range(QUAD):
            stop = (layers - 1) * span + (i + 1) * length
            start = (layers - 1 - back) * span
            windowed = stop - length - WINDOW >= start
            if windowed:
                start = stop - length - WINDOW
            scores = lax.dot_general(
                q_scr[s, i],
                k_scr[s, start:stop],
                (((1,), (1,)), ((), ())),
                preferred_element_type=F32,
            )
            weights = jnp.exp(scores)
            blocks = [weights[:, :-length], jnp.where(column <= row, weights[:, -length:], 0.0)]
            if windowed:
                blocks[0] = jnp.concatenate(
                    [jnp.where(column > row, weights[:, :length], 0.0), blocks[0][:, length:]], axis=1
                )
            if blocks[0].shape[1] == 0:
                blocks = blocks[1:]
            weights = jnp.concatenate(blocks, axis=1)
            total = jnp.sum(weights, axis=-1, keepdims=True)
            out = jnp.dot(weights.astype(BF16), v_scr[s, start:stop], preferred_element_type=F32)
            out = (out / total).astype(BF16)
            for h in range(heads):
                o_scr[i, s * length : (s + 1) * length, h * HD : (h + 1) * HD] = out[
                    h * length : (h + 1) * length
                ]

    for s in range(seqs):
        load(s)
    for back in range(layers):
        here = layer == back if back < layers - 1 else layer >= back

        @pl.when(here)
        def _():
            for s in range(seqs):
                attend(back, s)

    for m in range(QUAD):
        outs[m][...] = o_scr[r ^ m]


def attend(qs, kvs, chunk, chunks, first):
    length = kvs[0][0].shape[1]
    width = qs[0].shape[1] // chunks
    seqs, layers = len(kvs), len(kvs[0])
    rows = seqs * length
    heads = width // HD
    place = first // seqs
    return pl.pallas_call(
        functools.partial(attend_kernel, layers, seqs),
        grid=(1,),
        in_specs=[pl.BlockSpec((rows, width), lambda i: (place, chunk))] * QUAD
        + [pl.BlockSpec((QUAD, length, 2 * HD), lambda i: (0, 0, 0))] * (layers * seqs),
        out_specs=[pl.BlockSpec((rows, width), lambda i: (0, 0))] * QUAD,
        out_shape=[jax.ShapeDtypeStruct((rows, width), BF16)] * QUAD,
        scratch_shapes=[
            pltpu.VMEM((seqs, QUAD, heads * length, HD), BF16),
            pltpu.VMEM((seqs, layers * QUAD * length, HD), BF16),
            pltpu.VMEM((seqs, layers * QUAD * length, HD), BF16),
            pltpu.VMEM((QUAD, rows, width), BF16),
        ],
        cost_estimate=COST,
        compiler_params=params(24, 1),
        name="attend",
    )(*qs, *[block for kv in kvs for block in kv])


def assemble_kernel(chunks, places, *refs):
    out, r = refs[-1], place_in_quad()
    for n, (a, s) in enumerate(places):
        for m in range(QUAD):
            block = refs[n * QUAD + m]
            rows, width = block.shape
            at = pl.multiple_of(((r ^ m) * chunks + a) * width, width)
            out[s : s + rows, pl.ds(at, width)] = block[...]


def assemble(slots, chunks, seqs, length):
    places, a, s = [], 0, 0
    for group in slots:
        places.append((a, s))
        s += group[0].shape[0]
        if s == seqs * length:
            a, s = a + 1, 0
    width = slots[0][0].shape[1]
    slots = [block for group in slots for block in group]
    return pl.pallas_call(
        functools.partial(assemble_kernel, chunks, places),
        in_specs=[VMEM] * len(slots),
        out_specs=VMEM,
        out_shape=jax.ShapeDtypeStruct((seqs * length, QUAD * chunks * width), BF16),
        cost_estimate=COST,
        compiler_params=params(16),
        name="assemble",
    )(*slots)


def body(hidden, queries, input_gain, kv_weight, query_gain, key_gain):
    seqs, length, model_width = hidden.shape
    shard_rows, kv_width = kv_weight.shape
    devices = lax.axis_size("ctx")
    layers_total = devices // QUAD
    chunks = kv_width // 2 // HD // QUAD
    back_layers = WINDOW // (QUAD * length)
    rows = seqs * length

    me = lax.axis_index("ctx")
    r, layer = me % QUAD, me // QUAD

    def in_quad(block, m):
        return lax.ppermute(block, "ctx", [(i, i ^ m) for i in range(devices)])

    def other_core(block):
        return lax.ppermute(block, "dp", [(0, 1), (1, 0)])

    def layer_up(block):
        return lax.ppermute(block, "ctx", [(i, (i + QUAD) % devices) for i in range(devices)])

    ring = list(range(1, layers_total, 2))
    ring = [0] + ring + [i for i in range(layers_total - 1, 0, -1) if i % 2 == 0]
    place = {at: n for n, at in enumerate(ring)}
    ring_route = [
        (ring[n] * QUAD + q, ring[(n + 1) % layers_total] * QUAD + q)
        for n in range(layers_total)
        for q in range(QUAD)
    ]
    in_ring = shard_rows % 16 == 0 and layers_total <= 4
    origin = [
        [ring[(place[at] - k) % layers_total] for k in range(layers_total)]
        for at in range(layers_total)
    ]

    def exchange(slots):
        return [slots[0]] + [in_quad(slots[m], m) for m in range(1, QUAD)]

    def together(values):
        return list(lax.optimization_barrier(values))

    cut = cut_weights(kv_weight, chunks, 0)

    if in_ring:
        rings = [[own] for own in cut]
        for _ in range(layers_total - 1):
            for pieces in rings:
                pieces.append(lax.ppermute(pieces[-1], "ctx", ring_route))
    else:
        lines = [[i * QUAD + q for i in range(layers_total)] for q in range(QUAD)]
        rings = [
            [lax.all_gather(own, "ctx", axis=0, tiled=True, axis_index_groups=lines)]
            for own in cut
        ]

    def both_sides(a):
        if in_ring:
            return rings[a] + [cut_other[a], other_core(jnp.concatenate(rings[a][1:], axis=0))]
        other = other_core(rings[a][0])
        return rings[a] + [other, other]

    x = norm_slices(hidden, input_gain, shard_rows)

    slots = jnp.arange(QUAD, dtype=jnp.int32)
    own, slots, queries, w = together((x[0], slots, queries, kv_weight))
    cut_other = cut_weights(w, chunks, 1)
    x = [own] + exchange(x)[1:]
    slot_start = (layer * QUAD + (r ^ slots)) * length
    positions = (slot_start[:, None] + jnp.arange(length, dtype=jnp.int32)).reshape(-1)
    cos, sin = rotary_tables(positions, HD)
    cos, sin = cos.reshape(QUAD, length, HD), sin.reshape(QUAD, length, HD)
    q = query_slots(queries.reshape(rows, -1), query_gain, cos[0], sin[0], seqs)
    early = [pieces[: max(1, len(pieces) - 1)] for pieces in rings[1:]]

    def after(value, *others):
        return list(lax.optimization_barrier((value, others)))[0]

    x, rings[0], cos, sin, q = together((x, rings[0], cos, sin, q))
    x = after(x, early)

    def project_chunk(weights):
        return [
            list(project(x, weights, seqs, s, model_width // QUAD, origin)) for s in range(seqs)
        ]

    total = chunks * seqs
    parts = project_chunk(both_sides(0))
    sent = [exchange(part) for part in parts]
    for a in range(1, chunks):
        parts += project_chunk(both_sides(a))
    sent[0] = after(sent[0], parts[seqs:])

    kvs, outs = [], []
    for n in range(total):
        if n >= 1:
            sent[n] = after(sent[n], kvs[n - 1][1])
        if 2 <= n < total - 1:
            sent[n] = after(sent[n], kvs[n - 2])
        kv = reduce_parts(sent[n], key_gain, cos, sin)
        if n + seqs < total:
            sent.append(exchange(after(parts[n + seqs], kv)))
        kv = [kv]
        for _ in range(back_layers):
            kv.append(layer_up(kv[-1]))
        kvs.append(kv)
    q = exchange(after(q, sent[2]))
    for a in range(chunks - 1):
        out = attend(q, kvs[a * seqs : (a + 1) * seqs], a, chunks, 0)
        outs.append(exchange(out))
    outs.append(exchange(attend(q, kvs[-seqs:], chunks - 1, chunks, 0)))
    return assemble(outs, chunks, seqs, length).reshape(seqs, length, -1)


def solution(mesh):
    return jax.shard_map(
        body,
        mesh=mesh,
        in_specs=(P("dp", "ctx", None), P("dp", "ctx", None), P(), P("ctx", None), P(), P()),
        out_specs=P("dp", "ctx", None),
        check_vma=False,
    )
```
